128 devices in a mesh: walker: 8 (over x_lo, y), vec: 16 (over x_hi, z, core).
Axes of the slice: x: 4 (x_hi: 2, x_lo: 2; x = x_hi * 2 + x_lo), y: 4, z: 4, core: 2. Of those that a mesh axis runs over, the one named last changes fastest.
Arguments:
- walkers: bfloat16 [512, 128, 1024], P(('walker', 'vec')), may hold values from -6 to 6
- propagator: bfloat16 [1024, 1024], replicated, may hold values from -0.1875 to 0.1875
- chol: bfloat16 [128, 128, 1024], P('vec'), may hold values from -0.1875 to 0.1875
- parent_group: int32 [8, 16, 4], P(None, 'vec'), may hold values from 0 to 7, as said below
- parent_slot: int32 [8, 16, 4], P(None, 'vec'), may hold values from 0 to 3
- live_count: int32 [8, 16], P('walker', 'vec'), may hold values from 1 to 4, as said below
Outputs:
- new_walkers: bfloat16 [512, 128, 1024], P(('walker', 'vec'))
- energy: float32 [8, 16, 4], P('walker', 'vec')
The draws below stay inside these ranges and needn't reach their ends.
Inputs may be any that keep to these rules, and one draw needn't show every extreme that they name: For each d and b the 4 entries parent_group[d, b, :] are different groups. `live_count`: some device has all 4 slots live.
All inputs are finite; a program needn't handle non-finite values.
Results may differ from the reference program's by a relative error of at most 0.0047.
Values may be sent and summed in bfloat16 or wider, within the bound.
A program may use at most 192 MiB of HBM per device.

```python
import jax
import jax.numpy as jnp
from jax import lax

NEL = 128
NORB = 1024
W_DEV = 4
NCHOL = 128
NW_TOT = 512
N_WALKER = 8
N_VEC = 16


def draw_parent_group(key, part):
    keys = jax.random.split(jax.random.fold_in(key, 11), N_WALKER * N_VEC)
    perms = jax.vmap(lambda one: jax.random.permutation(one, N_WALKER))(keys)
    return perms[:, :W_DEV].reshape(N_WALKER, N_VEC, W_DEV).astype(jnp.int32)


def draw_live_count(key, part):
    counts = jax.random.randint(jax.random.fold_in(key, 23), (N_WALKER, N_VEC), 1, W_DEV + 1)
    return counts.at[0, 0].set(W_DEV).astype(jnp.int32)


def set_ends(drawn, stream_key, least, top_value):
    longest = drawn.shape.index(max(drawn.shape))
    spots = []
    for shift in (0, 1):
        where = [jax.random.randint(jax.random.fold_in(stream_key, axis), (), 0, length) for axis, length in enumerate(drawn.shape)]
        where[longest] = (where[longest] + shift) % drawn.shape[longest]
        spots.append(tuple(where))
    return drawn.at[spots[0]].set(least).at[spots[1]].set(top_value)


def levels(rng, dims, cuts, least, high):
    loudness = 1.0
    for dim, parts in cuts:
        draws = jax.random.uniform(jax.random.fold_in(jax.random.fold_in(rng, 6), dim), (parts,), jnp.float32, least / len(cuts), high / len(cuts))
        loudness = loudness * jnp.repeat(jnp.exp(draws), dims[dim] // parts).reshape((-1,) + (1,) * (len(dims) - 1 - dim))
    return loudness


def bell_draw(rng, extent, scale, bound, cuts=(), kind=jnp.bfloat16):
    loudness = levels(rng, extent, cuts, -0.22, 0.18) if cuts else 1.0
    drawn = jax.random.normal(rng, extent, jnp.float32) * scale * loudness
    return jnp.minimum(jnp.maximum(drawn, -bound), bound).astype(kind)


def setup_inputs(seed: int = 0) -> dict:
    seeds = jax.random.split(jax.random.key(seed), 7)
    return {
        "walkers": bell_draw(seeds[0], (NW_TOT, NEL, NORB), 1.0, 6.0, ((0, 128),)),
        "propagator": bell_draw(seeds[1], (NORB, NORB), NORB ** -0.5, 0.1875),
        "chol": bell_draw(seeds[2], (NCHOL, NEL, NORB), NORB ** -0.5, 0.1875, ((0, 16),)),
        "parent_group": draw_parent_group(jax.random.fold_in(seeds[6], 71), 0),
        "parent_slot": set_ends(jax.random.randint(seeds[4], (N_WALKER, N_VEC, W_DEV), 0, W_DEV), jax.random.fold_in(seeds[4], 1), 0, W_DEV - 1).astype(jnp.int32),
        "live_count": draw_live_count(jax.random.fold_in(seeds[6], 71), 0),
    }


def walker_energy(single, flat_chol):
    prod = jnp.dot(flat_chol, single.astype(jnp.float32).T).reshape(NCHOL, NEL, NEL)
    trace = jnp.trace(prod, axis1=1, axis2=2)
    cross = jnp.einsum('gij,gji->', prod, prod)
    return 0.5 * (jnp.sum(trace * trace) - cross) / (NCHOL * NEL)


def reference(walkers, propagator, chol, parent_group, parent_slot, live_count):
    moved = jnp.dot(walkers.reshape(-1, NORB), propagator, preferred_element_type=jnp.float32)
    moved = moved.astype(jnp.bfloat16).reshape(N_WALKER, N_VEC, W_DEV, NEL, NORB)
    column = jnp.arange(N_VEC, dtype=jnp.int32)[None, :, None]
    picked = moved[parent_group, column, parent_slot]
    keep = jnp.arange(W_DEV, dtype=jnp.int32)[None, None, :] < live_count[:, :, None]
    fresh = jnp.where(keep[..., None, None], picked, jnp.zeros_like(picked))
    flat_new = fresh.reshape(NW_TOT, NEL, NORB)
    flat_chol = chol.reshape(NCHOL * NEL, NORB).astype(jnp.float32)
    energy = lax.map(lambda single: walker_energy(single, flat_chol), flat_new)
    return flat_new, energy.reshape(N_WALKER, N_VEC, W_DEV)
```

```python
import jax
import jax.numpy as jnp
from jax import lax
from jax.experimental import pallas as pl
from jax.experimental.pallas import tpu as pltpu
from jax.sharding import PartitionSpec as P

MESH = pl.DeviceIdType.MESH
BLOCKS = 32
RELATIONS = [(across, along) for across in range(2) for along in range(4)]


def block_of(step):
    octet = step % 2
    pair = step // 2
    octet = jnp.where(step < 4, step // 2, octet)
    pair = jnp.where(step < 4, step % 2, pair)
    for first, last, kind, value in (
        (10, 15, "octet", 2),
        (15, 18, "pair", 5),
        (18, 24, "octet", 3),
        (24, 28, "pair", 6),
        (28, 32, "pair", 7),
    ):
        inside = (step >= first) & (step < last)
        octet = jnp.where(inside, value if kind == "octet" else step - first, octet)
        pair = jnp.where(inside, value if kind == "pair" else step - first, pair)
    return octet, pair


def kernel(
    groups, places, live, walkers_hbm, prop_hbm, chol_hbm, new_hbm, energy_ref,
    raw, prop, moved, wz, cv, outbox, inbox, fresh, ta, tb, da, db, acc,
    totals, parts, own_e, all_e, load_sem, send_sem, recv_sem,
):
    walker = lax.axis_index("walker")
    vec = lax.axis_index("vec")
    xl, y = walker // 4, walker % 4
    xh, z, core = vec // 8, (vec // 2) % 4, vec % 2

    def at(xl=xl, y=y, xh=xh, z=z, core=core):
        return (xl * 4 + y, (xh * 4 + z) * 2 + core)

    sibling = at(core=1 - core)
    hi = at(xl=1 - xl, xh=1 - xh)
    lo = at(xl=1 - xl)
    z_up, z_down, z_far = at(z=(z + 1) % 4), at(z=(z + 3) % 4), at(z=(z + 2) % 4)
    y_up, y_down = at(y=(y + 1) % 4), at(y=(y + 3) % 4)
    related = [
        at(xl=(xl + across) % 2, y=(y + along) % 4) for across, along in RELATIONS
    ]

    barrier = pltpu.get_barrier_semaphore()
    partners = [sibling, hi, z_up, z_down, z_far] + related[1:]
    for partner in partners:
        pl.semaphore_signal(barrier, inc=1, device_id=partner, device_id_type=MESH)

    load_prop = pltpu.make_async_copy(prop_hbm, prop, load_sem.at[0])
    load_raw = pltpu.make_async_copy(walkers_hbm, raw, load_sem.at[1])
    load_chol = pltpu.make_async_copy(chol_hbm, cv.at[pl.ds(0, 8)], load_sem.at[2])
    load_raw.start()
    load_prop.start()
    load_chol.start()

    table = {}

    def route(name, source, target, device):
        table[name] = (len(table), source, target, device)

    first = (1 - xl) + 2 * (y % 2)
    second = 3 - first
    route("core", chol_hbm, cv.at[pl.ds(8, 8)], sibling)
    for k, (source, slot) in enumerate(
        ((2 * first, 16), (2 * first + 1, 17), (2 * second, 24), (2 * second + 1, 25))
    ):
        route(f"hi{k}", chol_hbm.at[pl.ds(source, 1)], cv.at[pl.ds(slot, 1)], hi)
    route("lo0", cv.at[pl.ds(16, 1)], cv.at[pl.ds(18, 1)], lo)
    route("lo1", cv.at[pl.ds(17, 1)], cv.at[pl.ds(26, 1)], lo)
    route("y0", cv.at[pl.ds(16, 1)], cv.at[pl.ds(19, 1)], y_up)
    route("y1", cv.at[pl.ds(17, 1)], cv.at[pl.ds(27, 1)], y_down)
    for slot in (16, 17, 18, 19, 24, 25, 26, 27):
        route(f"sib{slot}", cv.at[pl.ds(slot, 1)], cv.at[pl.ds(slot + 4, 1)], sibling)
    for k in range(4):
        route(f"up{k}", moved.at[pl.ds(k, 1)], wz.at[pl.ds(4 + 2 * k, 1)], z_up)
        route(f"down{k}", moved.at[pl.ds((k + 1) % 4, 1)], wz.at[pl.ds(5 + 2 * k, 1)], z_down)
    for k in range(2):
        route(f"up{k + 4}", wz.at[pl.ds(4 + 2 * k, 1)], wz.at[pl.ds(12 + 2 * k, 1)], z_up)
        route(f"down{k + 4}", wz.at[pl.ds(7 + 2 * k, 1)], wz.at[pl.ds(13 + 2 * k, 1)], z_down)
    for r in range(1, 8):
        route(f"branch{r}", outbox.at[pl.ds(r, 1)], inbox.at[pl.ds(r, 1)], related[r])
    for k, device in enumerate((z_up, z_down, z_far)):
        route(f"part{k}", totals, parts.at[k], device)
    for r in range(1, 8):
        route(f"energy{r}", own_e, all_e.at[r], related[r])

    def copy(name):
        index, source, target, device = table[name]
        return pltpu.make_async_remote_copy(
            src_ref=source,
            dst_ref=target,
            send_sem=send_sem.at[index],
            recv_sem=recv_sem.at[index],
            device_id=device,
            device_id_type=MESH,
        )

    def start(*names):
        for name in names:
            copy(name).start()

    def arrived(*names):
        for name in names:
            copy(name).wait_recv()

    acc[...] = jnp.zeros_like(acc)
    inbox[8] = jnp.zeros_like(inbox[8])

    pl.semaphore_wait(barrier, len(partners))
    start("hi0", "hi1", "hi2", "hi3", "core")

    load_raw.wait()
    load_prop.wait()

    def propagate(base):
        rows = raw[base : base + 2].reshape(256, 1024)

        @pl.loop(0, 4)
        def _(tile):
            columns = pl.ds(pl.multiple_of(tile * 256, 256), 256)
            out = jnp.dot(rows, prop[:, columns], preferred_element_type=jnp.float32)
            out = out.astype(jnp.bfloat16).reshape(2, 128, 256)
            moved[base : base + 2, :, columns] = out
            wz[base : base + 2, :, columns] = out

    propagate(0)
    start("up0", "down0", "up1")
    propagate(2)
    start("down1", "up2", "down2", "up3", "down3")

    def choose(r):
        across, along = RELATIONS[r]
        other = ((xl + across) % 2) * 4 + (y + along) % 4
        slot = 0
        for k in range(4):
            slot = slot + jnp.where(groups[other, 0, k] == walker, places[other, 0, k], 0)
        return moved[slot]

    for r in (4, 1, 3, 5):
        outbox[r] = choose(r)
        start(f"branch{r}")
    for r in (2, 6, 7):
        outbox[r] = choose(r)
    inbox[0] = choose(0)

    load_chol.wait()

    def multiply(step, t):
        octet, pair = block_of(step)
        vectors = cv[pl.ds(octet * 8, 8)].reshape(1024, 1024)
        block = wz[pl.ds(pair * 2, 2)].reshape(256, 1024)
        t[...] = lax.dot_general(
            vectors, block, (((1,), (1,)), ((), ())), preferred_element_type=jnp.float32
        )

    row = lax.broadcasted_iota(jnp.int32, (8, 128), 0)
    lane = lax.broadcasted_iota(jnp.int32, (8, 128), 1)

    def reduce(step, t, diagonal):
        _, pair = block_of(step)
        crosses = []
        for w in range(2):
            cross = None
            for g in range(8):
                block = t[g * 128 : (g + 1) * 128, w * 128 : (w + 1) * 128]
                turned = block.astype(jnp.bfloat16).T.astype(jnp.float32)
                one = jnp.sum((block * turned).reshape(16, 8, 128), axis=0)
                cross = one if cross is None else cross + one
                found = jnp.where(lane == row, block[0:8], 0.0)
                for k in range(1, 16):
                    found = jnp.where(lane == row + 8 * k, block[8 * k : 8 * k + 8], found)
                diagonal[(w * 8 + g) * 8 : (w * 8 + g) * 8 + 8, :] = found
            crosses.append(cross)
        lines = diagonal[pl.ds(0, 16, stride=8), :]
        for k in range(1, 8):
            lines = lines + diagonal[pl.ds(k, 16, stride=8), :]
        trace = jnp.sum(lines, axis=1, keepdims=True)
        squares = jnp.where(lax.broadcasted_iota(jnp.int32, (16, 128), 1) == 0, trace * trace, 0.0)
        for w in range(2):
            rows = pl.ds(pl.multiple_of((pair * 2 + w) * 8, 8), 8)
            acc[rows, :] = acc[rows, :] + squares[w * 8 : w * 8 + 8] - crosses[w]

    def branch_in():
        arrived(*[f"branch{r}" for r in range(1, 8)])
        count = live[0, 0]
        for k in range(4):
            group = groups[walker, 0, k]
            r = ((group >> 2) ^ xl) * 4 + ((y - (group & 3)) & 3)
            fresh[k] = inbox[jnp.where(k < count, r, 8)]
        pltpu.make_async_copy(fresh, new_hbm, load_sem.at[3]).start()

    def serve(step):
        @pl.when(step == 2)
        def _():
            arrived("core")

        @pl.when(step == 4)
        def _():
            arrived("up0", "hi0")
            start("up4", "sib16", "lo0", "y0")
            arrived("down0")

        @pl.when(step == 6)
        def _():
            arrived("up1", "down1", "hi1")
            start("up5", "down4", "sib17", "lo1", "y1")
            start("branch2", "branch6", "branch7")

        @pl.when(step == 8)
        def _():
            arrived("up2", "down2", "hi2")
            start("down5", "sib24")
            arrived("y0", "lo0")
            start("sib18", "sib19")

        @pl.when(step == 10)
        def _():
            arrived("sib16", "sib17", "sib18", "sib19")

        @pl.when(step == 18)
        def _():
            arrived("sib24", "sib25", "sib26", "sib27")

        @pl.when(step == 24)
        def _():
            arrived("up4", "down4")

        @pl.when(step == 28)
        def _():
            branch_in()
            arrived("up5", "down5")

    def serve_odd(step):
        @pl.when(step == 15)
        def _():
            arrived("up3", "down3", "hi3")
            start("sib25")
            arrived("y1", "lo1")
            start("sib26", "sib27")

    multiply(0, ta)

    def body(i, carry):
        step = 2 * i
        serve_odd(step + 1)
        multiply(step + 1, tb)
        reduce(step, ta, da)
        serve(step + 2)
        multiply(step + 2, ta)
        reduce(step + 1, tb, db)
        return carry

    lax.fori_loop(0, BLOCKS // 2 - 1, body, 0)
    multiply(BLOCKS - 1, tb)
    reduce(BLOCKS - 2, ta, da)
    reduce(BLOCKS - 1, tb, db)

    sums = acc[pl.ds(0, 16, stride=8), :]
    for k in range(1, 8):
        sums = sums + acc[pl.ds(k, 16, stride=8), :]
    totals[...] = sums
    start("part0", "part1", "part2")
    own_e[...] = jnp.zeros_like(own_e)
    arrived("part0", "part1", "part2")
    for k in range(4):
        below, above, far = 4 + 2 * k, 5 + 2 * ((k + 3) % 4), 12 + (0, 2, 1, 3)[k]
        own_e[k : k + 1, :] = (
            totals[k : k + 1, :]
            + parts[1, below : below + 1, :]
            + parts[0, above : above + 1, :]
            + parts[2, far : far + 1, :]
        )
    own_e[...] = jnp.broadcast_to(jnp.sum(own_e[...], axis=1, keepdims=True), (8, 128))
    names = [f"energy{r}" for r in range(1, 8)]
    start(*names)
    all_e[0] = own_e[...]
    arrived(*names)
    count = live[0, 0]
    result = jnp.zeros((1, 128), jnp.float32)
    for k in range(4):
        group = groups[walker, 0, k]
        r = ((group >> 2) ^ xl) * 4 + ((y - (group & 3)) & 3)
        tile = all_e[r]
        value = jnp.sum(jnp.where(row == places[walker, 0, k], tile, 0.0), axis=0, keepdims=True)
        chosen = (lane[0:1] == k) & (count > k)
        result = jnp.where(chosen, value * (0.5 / 16384), result)
    energy_ref[0] = result[:, 0:4]

    for name in table:
        copy(name).wait_send()
    pltpu.make_async_copy(fresh, new_hbm, load_sem.at[3]).wait()


def on_device(walkers, propagator, chol, parent_group, parent_slot, live_count):
    bf16, f32 = jnp.bfloat16, jnp.float32
    slot = (128, 1024)
    smem = pl.BlockSpec(memory_space=pltpu.SMEM)
    anywhere = pl.BlockSpec(memory_space=pl.ANY)
    routes = 48
    return pl.pallas_call(
        kernel,
        out_shape=(
            jax.ShapeDtypeStruct((4,) + slot, bf16),
            jax.ShapeDtypeStruct((1, 1, 4), f32),
        ),
        in_specs=[smem, smem, smem, anywhere, anywhere, anywhere],
        out_specs=(anywhere, pl.BlockSpec(memory_space=pltpu.VMEM)),
        scratch_shapes=[
            pltpu.VMEM((4,) + slot, bf16),
            pltpu.VMEM((1024, 1024), bf16),
            pltpu.VMEM((4,) + slot, bf16),
            pltpu.VMEM((16,) + slot, bf16),
            pltpu.VMEM((32,) + slot, bf16),
            pltpu.VMEM((8,) + slot, bf16),
            pltpu.VMEM((9,) + slot, bf16),
            pltpu.VMEM((4,) + slot, bf16),
            pltpu.VMEM((1024, 256), f32),
            pltpu.VMEM((1024, 256), f32),
            pltpu.VMEM((128, 128), f32),
            pltpu.VMEM((128, 128), f32),
            pltpu.VMEM((128, 128), f32),
            pltpu.VMEM((16, 128), f32),
            pltpu.VMEM((3, 16, 128), f32),
            pltpu.VMEM((8, 128), f32),
            pltpu.VMEM((8, 8, 128), f32),
            pltpu.SemaphoreType.DMA((4,)),
            pltpu.SemaphoreType.DMA((routes,)),
            pltpu.SemaphoreType.DMA((routes,)),
        ],
        compiler_params=pltpu.CompilerParams(
            collective_id=0, has_side_effects=True, vmem_limit_bytes=48 << 20
        ),
        cost_estimate=pl.CostEstimate(
            flops=2 * (512 * 128 * 128 * 1024 + 512 * 1024 * 1024),
            bytes_accessed=8 << 20,
            transcendentals=0,
        ),
        name="propagate_branch_energy",
    )(parent_group, parent_slot, live_count, walkers, propagator, chol)


def solution(mesh):
    in_specs = (
        P(("walker", "vec"), None, None),
        P(),
        P("vec", None, None),
        P(None, "vec", None),
        P(None, "vec", None),
        P("walker", "vec"),
    )
    out_specs = (P(("walker", "vec"), None, None), P("walker", "vec", None))
    return jax.shard_map(
        on_device, mesh=mesh, in_specs=in_specs, out_specs=out_specs, check_vma=False
    )
```

```python
import jax
import jax.numpy as jnp
from jax import lax
from jax.experimental import pallas as pl
from jax.experimental.pallas import tpu as pltpu
from jax.sharding import PartitionSpec as P

MESH = pl.DeviceIdType.MESH
BLOCKS = 32
RELATIONS = [(across, along) for across in range(2) for along in range(4)]


def block_of(step):
    octet = step % 2
    pair = step // 2
    octet = jnp.where(step < 4, step // 2, octet)
    pair = jnp.where(step < 4, step % 2, pair)
    for first, last, kind, value in (
        (10, 15, "octet", 2),
        (15, 18, "pair", 5),
        (18, 24, "octet", 3),
        (24, 28, "pair", 6),
        (28, 32, "pair", 7),
    ):
        inside = (step >= first) & (step < last)
        octet = jnp.where(inside, value if kind == "octet" else step - first, octet)
        pair = jnp.where(inside, value if kind == "pair" else step - first, pair)
    return octet, pair


def kernel(
    groups_hbm, places_hbm, live_hbm, walkers_hbm, prop_hbm, chol_hbm, new_hbm, energy_ref,
    groups, places, live,
    raw, prop, moved, wz, cv, outbox, inbox, fresh, ta, tb, da, db, acc,
    totals, parts, own_e, all_e, last, lasts, load_sem, send_sem, recv_sem,
):
    walker = lax.axis_index("walker")
    vec = lax.axis_index("vec")
    xl, y = walker // 4, walker % 4
    xh, z, core = vec // 8, (vec // 2) % 4, vec % 2

    def at(xl=xl, y=y, xh=xh, z=z, core=core):
        return (xl * 4 + y, (xh * 4 + z) * 2 + core)

    sibling = at(core=1 - core)
    hi = at(xl=1 - xl, xh=1 - xh)
    lo = at(xl=1 - xl)
    z_up, z_down, z_far = at(z=(z + 1) % 4), at(z=(z + 3) % 4), at(z=(z + 2) % 4)
    y_up, y_down = at(y=(y + 1) % 4), at(y=(y + 3) % 4)
    related = [
        at(xl=(xl + across) % 2, y=(y + along) % 4) for across, along in RELATIONS
    ]

    beyond = [
        at(xl=(xl + across) % 2, y=(y + along) % 4, z=(z + 2) % 4) for across, along in RELATIONS
    ]

    barrier = pltpu.get_barrier_semaphore()
    partners = [sibling, hi, z_up, z_down] + related[1:] + beyond
    for partner in partners:
        pl.semaphore_signal(barrier, inc=1, device_id=partner, device_id_type=MESH)

    small = [
        pltpu.make_async_copy(source, target, load_sem.at[4 + k])
        for k, (source, target) in enumerate(
            ((groups_hbm, groups), (places_hbm, places), (live_hbm, live))
        )
    ]
    load_prop = pltpu.make_async_copy(prop_hbm, prop, load_sem.at[0])
    load_raw = pltpu.make_async_copy(walkers_hbm, raw, load_sem.at[1])
    load_chol = pltpu.make_async_copy(chol_hbm, cv.at[pl.ds(0, 8)], load_sem.at[2])
    load_raw.start()
    load_prop.start()
    for load in small:
        load.start()
    load_chol.start()

    table = {}

    def route(name, source, target, device):
        table[name] = (len(table), source, target, device)

    first = (1 - xl) + 2 * (y % 2)
    second = 3 - first
    route("core", chol_hbm, cv.at[pl.ds(8, 8)], sibling)
    for k, (source, slot) in enumerate(
        ((2 * first, 16), (2 * first + 1, 17), (2 * second, 24), (2 * second + 1, 25))
    ):
        route(f"hi{k}", chol_hbm.at[pl.ds(source, 1)], cv.at[pl.ds(slot, 1)], hi)
    route("lo0", cv.at[pl.ds(16, 1)], cv.at[pl.ds(18, 1)], lo)
    route("lo1", cv.at[pl.ds(17, 1)], cv.at[pl.ds(26, 1)], lo)
    route("y0", cv.at[pl.ds(16, 1)], cv.at[pl.ds(19, 1)], y_up)
    route("y1", cv.at[pl.ds(17, 1)], cv.at[pl.ds(27, 1)], y_down)
    for slot in (16, 17, 18, 19, 24, 25, 26, 27):
        route(f"sib{slot}", cv.at[pl.ds(slot, 1)], cv.at[pl.ds(slot + 4, 1)], sibling)
    for k in range(4):
        route(f"up{k}", moved.at[pl.ds(k, 1)], wz.at[pl.ds(4 + 2 * k, 1)], z_up)
        route(f"down{k}", moved.at[pl.ds((k + 1) % 4, 1)], wz.at[pl.ds(5 + 2 * k, 1)], z_down)
    for k in range(2):
        route(f"up{k + 4}", wz.at[pl.ds(4 + 2 * k, 1)], wz.at[pl.ds(12 + 2 * k, 1)], z_up)
        route(f"down{k + 4}", wz.at[pl.ds(7 + 2 * k, 1)], wz.at[pl.ds(13 + 2 * k, 1)], z_down)
    for r in range(1, 8):
        route(f"branch{r}", outbox.at[pl.ds(r, 1)], inbox.at[pl.ds(r, 1)], related[r])
    for k, device in enumerate((z_up, z_down, z_far)):
        route(f"part{k}", totals, parts.at[k], device)
    for r in range(1, 8):
        route(f"energy{r}", own_e, all_e.at[r], related[r])
    for r in range(8):
        route(f"last{r}", last, lasts.at[r], beyond[r])

    def copy(name):
        index, source, target, device = table[name]
        return pltpu.make_async_remote_copy(
            src_ref=source,
            dst_ref=target,
            send_sem=send_sem.at[index],
            recv_sem=recv_sem.at[index],
            device_id=device,
            device_id_type=MESH,
        )

    def start(*names):
        for name in names:
            copy(name).start()

    def arrived(*names):
        for name in names:
            copy(name).wait_recv()

    acc[...] = jnp.zeros_like(acc)
    inbox[8] = jnp.zeros_like(inbox[8])

    pl.semaphore_wait(barrier, len(partners))
    start("hi0", "hi1", "hi2", "hi3", "core")

    load_raw.wait()
    load_prop.wait()

    def propagate(base):
        rows = raw[base : base + 2].reshape(256, 1024)

        @pl.loop(0, 4)
        def _(tile):
            columns = pl.ds(pl.multiple_of(tile * 256, 256), 256)
            out = jnp.dot(rows, prop[:, columns], preferred_element_type=jnp.float32)
            out = out.astype(jnp.bfloat16).reshape(2, 128, 256)
            moved[base : base + 2, :, columns] = out
            wz[base : base + 2, :, columns] = out

    propagate(0)
    start("up0", "down0", "up1")
    propagate(2)
    start("down1", "up2", "down2", "up3", "down3")

    for load in small:
        load.wait()

    def choose(r):
        across, along = RELATIONS[r]
        other = ((xl + across) % 2) * 4 + (y + along) % 4
        slot = 0
        for k in range(4):
            slot = slot + jnp.where(groups[k, other] == walker, places[k, other], 0)
        return moved[slot]

    for r in (4, 1, 3, 5):
        outbox[r] = choose(r)
        start(f"branch{r}")
    for r in (2, 6, 7):
        outbox[r] = choose(r)
    inbox[0] = choose(0)

    load_chol.wait()

    def multiply(step, t):
        octet, pair = block_of(step)
        vectors = cv[pl.ds(octet * 8, 8)].reshape(1024, 1024)
        block = wz[pl.ds(pair * 2, 2)].reshape(256, 1024)
        t[...] = lax.dot_general(
            block, vectors, (((1,), (1,)), ((), ())), preferred_element_type=jnp.float32
        )

    row = lax.broadcasted_iota(jnp.int32, (8, 128), 0)
    lane = lax.broadcasted_iota(jnp.int32, (8, 128), 1)

    def reduce(step, t, diagonal):
        _, pair = block_of(step)
        crosses = []
        for w in range(2):
            cross = None
            for g in range(8):
                block = t[w * 128 : (w + 1) * 128, g * 128 : (g + 1) * 128]
                turned = block.astype(jnp.bfloat16).T.astype(jnp.float32)
                one = jnp.sum((block * turned).reshape(16, 8, 128), axis=0)
                cross = one if cross is None else cross + one
                found = jnp.where(lane == row, block[0:8], 0.0)
                for k in range(1, 16):
                    found = jnp.where(lane == row + 8 * k, block[8 * k : 8 * k + 8], found)
                diagonal[(w * 8 + g) * 8 : (w * 8 + g) * 8 + 8, :] = found
            crosses.append(cross)
        lines = diagonal[pl.ds(0, 16, stride=8), :]
        for k in range(1, 8):
            lines = lines + diagonal[pl.ds(k, 16, stride=8), :]
        trace = jnp.sum(lines, axis=1, keepdims=True)
        squares = jnp.where(lax.broadcasted_iota(jnp.int32, (16, 128), 1) == 0, trace * trace, 0.0)
        for w in range(2):
            rows = pl.ds(pl.multiple_of((pair * 2 + w) * 8, 8), 8)
            acc[rows, :] = acc[rows, :] + squares[w * 8 : w * 8 + 8] - crosses[w]

    def branch_in():
        arrived(*[f"branch{r}" for r in range(1, 8)])
        count = live[0, 0]
        for k in range(4):
            group = groups[k, walker]
            r = ((group >> 2) ^ xl) * 4 + ((y - (group & 3)) & 3)
            fresh[k] = inbox[jnp.where(k < count, r, 8)]
        pltpu.make_async_copy(fresh, new_hbm, load_sem.at[3]).start()

    def serve(step):
        @pl.when(step == 2)
        def _():
            arrived("core")

        @pl.when(step == 4)
        def _():
            arrived("up0", "hi0")
            start("up4", "sib16", "lo0", "y0")
            arrived("down0")

        @pl.when(step == 6)
        def _():
            arrived("up1", "down1", "hi1")
            start("up5", "down4", "sib17", "lo1", "y1")
            start("branch2", "branch6", "branch7")

        @pl.when(step == 8)
        def _():
            arrived("up2", "down2", "hi2")
            start("down5", "sib24")
            arrived("y0", "lo0")
            start("sib18", "sib19")

        @pl.when(step == 10)
        def _():
            arrived("sib16", "sib17", "sib18", "sib19")

        @pl.when(step == 18)
        def _():
            arrived("sib24", "sib25", "sib26", "sib27")

        @pl.when(step == 24)
        def _():
            arrived("up4", "down4")

        @pl.when(step == 14)
        def _():
            arrived("up3", "down3", "hi3")
            start("sib25")
            arrived("y1", "lo1")
            start("sib26", "sib27")

    multiply(0, ta)
    multiply(1, tb)
    reduce(0, ta, da)

    def body(i, carry):
        step = 2 * i
        serve(step)
        multiply(step, ta)
        reduce(step - 1, tb, db)
        multiply(step + 1, tb)
        reduce(step, ta, da)
        return carry

    def sublane_sums(base, count):
        sums = acc[pl.ds(base * 8, count, stride=8), :]
        for k in range(1, 8):
            sums = sums + acc[pl.ds(base * 8 + k, count, stride=8), :]
        return sums

    lax.fori_loop(1, BLOCKS // 2 - 2, body, 0)
    reduce(BLOCKS - 5, tb, db)
    totals[...] = sublane_sums(0, 16)
    start("part0", "part1", "part2")
    own_e[...] = jnp.zeros_like(own_e)
    last[...] = jnp.zeros_like(last)
    arrived("up5", "down5")
    multiply(BLOCKS - 4, ta)
    multiply(BLOCKS - 3, tb)
    reduce(BLOCKS - 4, ta, da)
    arrived("part0", "part1", "part2")
    for k in range(4):
        below, above = 4 + 2 * k, 5 + 2 * ((k + 3) % 4)
        line = totals[k : k + 1, :] + parts[1, below : below + 1, :] + parts[0, above : above + 1, :]
        if k % 2 == 0:
            line = line + parts[2, 12 + k // 2 : 13 + k // 2, :]
        own_e[k : k + 1, :] = line
    start(*[f"energy{r}" for r in range(1, 8)])
    multiply(BLOCKS - 2, ta)
    reduce(BLOCKS - 3, tb, db)
    multiply(BLOCKS - 1, tb)
    reduce(BLOCKS - 2, ta, da)
    reduce(BLOCKS - 1, tb, db)
    last[0:2, :] = sublane_sums(14, 2)
    start(*[f"last{r}" for r in range(8)])
    branch_in()
    all_e[0] = own_e[...]
    arrived(*[f"energy{r}" for r in range(1, 8)])
    arrived(*[f"last{r}" for r in range(8)])
    count = live[0, 0]
    result = jnp.zeros((1, 128), jnp.float32)
    for k in range(4):
        group, place = groups[k, walker], places[k, walker]
        r = ((group >> 2) ^ xl) * 4 + ((y - (group & 3)) & 3)
        late = jnp.where((place & 1) == 1, place >> 1, 8)
        tile = jnp.where(row == place, all_e[r], 0.0) + jnp.where(row == late, lasts[r], 0.0)
        value = jnp.sum(jnp.sum(tile, axis=0, keepdims=True), axis=1, keepdims=True)
        chosen = (lane[0:1] == k) & (count > k)
        result = jnp.where(chosen, value * (0.5 / 16384), result)
    energy_ref[0] = result[:, 0:4]

    for name in table:
        copy(name).wait_send()
    pltpu.make_async_copy(fresh, new_hbm, load_sem.at[3]).wait()


def on_device(walkers, propagator, chol, parent_group, parent_slot, live_count):
    bf16, f32 = jnp.bfloat16, jnp.float32
    slot = (128, 1024)
    anywhere = pl.BlockSpec(memory_space=pl.ANY)
    hbm = pl.BlockSpec(memory_space=pltpu.HBM)
    routes = 56
    return pl.pallas_call(
        kernel,
        out_shape=(
            jax.ShapeDtypeStruct((4,) + slot, bf16),
            jax.ShapeDtypeStruct((1, 1, 4), f32),
        ),
        in_specs=[hbm] * 6,
        out_specs=(anywhere, pl.BlockSpec(memory_space=pltpu.VMEM)),
        scratch_shapes=[
            pltpu.SMEM((4, 8), jnp.int32),
            pltpu.SMEM((4, 8), jnp.int32),
            pltpu.SMEM((1, 1), jnp.int32),
            pltpu.VMEM((4,) + slot, bf16),
            pltpu.VMEM((1024, 1024), bf16),
            pltpu.VMEM((4,) + slot, bf16),
            pltpu.VMEM((16,) + slot, bf16),
            pltpu.VMEM((32,) + slot, bf16),
            pltpu.VMEM((8,) + slot, bf16),
            pltpu.VMEM((9,) + slot, bf16),
            pltpu.VMEM((4,) + slot, bf16),
            pltpu.VMEM((256, 1024), f32),
            pltpu.VMEM((256, 1024), f32),
            pltpu.VMEM((128, 128), f32),
            pltpu.VMEM((128, 128), f32),
            pltpu.VMEM((128, 128), f32),
            pltpu.VMEM((16, 128), f32),
            pltpu.VMEM((3, 16, 128), f32),
            pltpu.VMEM((8, 128), f32),
            pltpu.VMEM((8, 8, 128), f32),
            pltpu.VMEM((8, 128), f32),
            pltpu.VMEM((8, 8, 128), f32),
            pltpu.SemaphoreType.DMA((7,)),
            pltpu.SemaphoreType.DMA((routes,)),
            pltpu.SemaphoreType.DMA((routes,)),
        ],
        compiler_params=pltpu.CompilerParams(
            collective_id=0, has_side_effects=True, vmem_limit_bytes=52 << 20
        ),
        cost_estimate=pl.CostEstimate(
            flops=2 * (512 * 128 * 128 * 1024 + 512 * 1024 * 1024),
            bytes_accessed=8 << 20,
            transcendentals=0,
        ),
        name="propagate_branch_energy",
    )(parent_group[:, 0, :].T, parent_slot[:, 0, :].T, live_count, walkers, propagator, chol)


def solution(mesh):
    in_specs = (
        P(("walker", "vec"), None, None),
        P(),
        P("vec", None, None),
        P(None, "vec", None),
        P(None, "vec", None),
        P("walker", "vec"),
    )
    out_specs = (P(("walker", "vec"), None, None), P("walker", "vec", None))
    return jax.shard_map(
        on_device, mesh=mesh, in_specs=in_specs, out_specs=out_specs, check_vma=False
    )
```

```python
import jax
import jax.numpy as jnp
from jax import lax
from jax.experimental import pallas as pl
from jax.experimental.pallas import tpu as pltpu
from jax.sharding import PartitionSpec as P

MESH = pl.DeviceIdType.MESH
BLOCKS = 32
RELATIONS = [(across, along) for across in range(2) for along in range(4)]


def block_of(step):
    octet = step % 2
    pair = step // 2
    octet = jnp.where(step < 4, step // 2, octet)
    pair = jnp.where(step < 4, step % 2, pair)
    for first, last, kind, value in (
        (10, 15, "octet", 2),
        (15, 18, "pair", 5),
        (18, 24, "octet", 3),
        (24, 28, "pair", 6),
        (28, 32, "pair", 7),
    ):
        inside = (step >= first) & (step < last)
        octet = jnp.where(inside, value if kind == "octet" else step - first, octet)
        pair = jnp.where(inside, value if kind == "pair" else step - first, pair)
    return octet, pair


def kernel(
    parents_hbm, live_hbm, walkers_hbm, prop_hbm, chol_hbm, new_hbm, energy_ref,
    parents, live,
    raw, early, prop, moved, wz, cv, outbox, inbox, fresh, ta, tb, t7, da, db, acc,
    totals, parts, own_e, all_e, last, lasts, load_sem, send_sem, recv_sem,
):
    walker = lax.axis_index("walker")
    vec = lax.axis_index("vec")
    xl, y = walker // 4, walker % 4
    xh, z, core = vec // 8, (vec // 2) % 4, vec % 2

    def at(xl=xl, y=y, xh=xh, z=z, core=core):
        return (xl * 4 + y, (xh * 4 + z) * 2 + core)

    sibling = at(core=1 - core)
    hi = at(xl=1 - xl, xh=1 - xh)
    lo = at(xl=1 - xl)
    z_up, z_down, z_far = at(z=(z + 1) % 4), at(z=(z + 3) % 4), at(z=(z + 2) % 4)
    y_up, y_down = at(y=(y + 1) % 4), at(y=(y + 3) % 4)
    related = [
        at(xl=(xl + across) % 2, y=(y + along) % 4) for across, along in RELATIONS
    ]

    beyond = [
        at(xl=(xl + across) % 2, y=(y + along) % 4, z=(z + 2) % 4) for across, along in RELATIONS
    ]

    barrier = pltpu.get_barrier_semaphore()
    partners = [sibling, hi, z_up, z_down] + related[1:] + beyond
    for partner in partners:
        pl.semaphore_signal(barrier, inc=1, device_id=partner, device_id_type=MESH)

    small = [
        pltpu.make_async_copy(source, target, load_sem.at[4 + k])
        for k, (source, target) in enumerate(
            ((parents_hbm, parents), (live_hbm, live))
        )
    ]
    load_prop = pltpu.make_async_copy(prop_hbm, prop, load_sem.at[0])
    load_raw = pltpu.make_async_copy(walkers_hbm, raw, load_sem.at[1])
    load_chol = pltpu.make_async_copy(chol_hbm, cv.at[pl.ds(0, 8)], load_sem.at[2])
    load_raw.start()
    load_prop.start()
    for load in small:
        load.start()
    load_chol.start()

    table = {}

    def route(name, source, target, device):
        table[name] = (len(table), source, target, device)

    first = (1 - xl) + 2 * (y % 2)
    second = 3 - first
    route("core", chol_hbm, cv.at[pl.ds(8, 8)], sibling)
    for k, (source, slot) in enumerate(
        ((2 * first, 16), (2 * first + 1, 17), (2 * second, 24), (2 * second + 1, 25))
    ):
        route(f"hi{k}", chol_hbm.at[pl.ds(source, 1)], cv.at[pl.ds(slot, 1)], hi)
    route("lo0", cv.at[pl.ds(16, 1)], cv.at[pl.ds(18, 1)], lo)
    route("lo1", cv.at[pl.ds(17, 1)], cv.at[pl.ds(26, 1)], lo)
    route("y0", cv.at[pl.ds(16, 1)], cv.at[pl.ds(19, 1)], y_up)
    route("y1", cv.at[pl.ds(17, 1)], cv.at[pl.ds(27, 1)], y_down)
    for slot in (16, 17, 18, 19, 24, 25, 26, 27):
        route(f"sib{slot}", cv.at[pl.ds(slot, 1)], cv.at[pl.ds(slot + 4, 1)], sibling)
    for k in range(4):
        if k == 0:
            route("up0", walkers_hbm.at[pl.ds(0, 1)], early.at[pl.ds(0, 1)], z_up)
            route("down0", walkers_hbm.at[pl.ds(1, 1)], early.at[pl.ds(1, 1)], z_down)
            continue
        route(f"up{k}", moved.at[pl.ds(k, 1)], wz.at[pl.ds(4 + 2 * k, 1)], z_up)
        route(f"down{k}", moved.at[pl.ds((k + 1) % 4, 1)], wz.at[pl.ds(5 + 2 * k, 1)], z_down)
    route("up4", wz.at[pl.ds(4, 1)], wz.at[pl.ds(12, 1)], z_up)
    route("down4", wz.at[pl.ds(7, 1)], wz.at[pl.ds(13, 1)], z_down)
    for part in range(2):
        half = pl.ds(part * 512, 512)
        route(f"up5{part}", wz.at[pl.ds(6, 1), :, half], wz.at[pl.ds(14, 1), :, half], z_up)
        route(f"down5{part}", wz.at[pl.ds(9, 1), :, half], wz.at[pl.ds(15, 1), :, half], z_down)
    for r in range(1, 8):
        route(f"branch{r}", outbox.at[pl.ds(r, 1)], inbox.at[pl.ds(r, 1)], related[r])
    for k, device in enumerate((z_up, z_down, z_far)):
        route(f"part{k}", totals, parts.at[k], device)
    for r in range(1, 8):
        route(f"energy{r}", own_e, all_e.at[r], related[r])
    for r in range(8):
        route(f"last{r}", last, lasts.at[r], beyond[r])

    def copy(name):
        index, source, target, device = table[name]
        return pltpu.make_async_remote_copy(
            src_ref=source,
            dst_ref=target,
            send_sem=send_sem.at[index],
            recv_sem=recv_sem.at[index],
            device_id=device,
            device_id_type=MESH,
        )

    def start(*names):
        for name in names:
            copy(name).start()

    def arrived(*names):
        for name in names:
            copy(name).wait_recv()

    acc[...] = jnp.zeros_like(acc)
    inbox[8] = jnp.zeros_like(inbox[8])

    pl.semaphore_wait(barrier, len(partners))
    start("up0", "down0", "hi0", "hi1", "hi2", "hi3", "core")

    load_raw.wait()
    load_prop.wait()

    def propagate(source, *targets):
        rows = source[...].reshape(256, 1024)

        @pl.loop(0, 4)
        def _(tile):
            columns = pl.ds(pl.multiple_of(tile * 256, 256), 256)
            out = jnp.dot(rows, prop[:, columns], preferred_element_type=jnp.float32)
            out = out.astype(jnp.bfloat16).reshape(2, 128, 256)
            for target in targets:
                target[:, :, columns] = out

    propagate(raw.at[0:2], moved.at[0:2], wz.at[0:2])
    start("up1")
    propagate(raw.at[2:4], moved.at[2:4], wz.at[2:4])
    start("down1", "up2", "down2", "up3", "down3")

    for load in small:
        load.wait()

    def choose(r):
        across, along = RELATIONS[r]
        other = ((xl + across) % 2) * 4 + (y + along) % 4
        slot = 0
        for k in range(4):
            parent = parents[k, other]
            slot = slot + jnp.where(parent >> 2 == walker, parent & 3, 0)
        return moved[slot]

    for r in (4, 1, 3):
        outbox[r] = choose(r)
        start(f"branch{r}")
    for r in (2, 5, 6, 7):
        outbox[r] = choose(r)
    inbox[0] = choose(0)

    load_chol.wait()

    def multiply(step, t):
        octet, pair = block_of(step)
        vectors = cv[pl.ds(octet * 8, 8)].reshape(1024, 1024)
        block = wz[pl.ds(pair * 2, 2)].reshape(256, 1024)
        t[...] = lax.dot_general(
            block, vectors, (((1,), (1,)), ((), ())), preferred_element_type=jnp.float32
        )

    row = lax.broadcasted_iota(jnp.int32, (8, 128), 0)
    lane = lax.broadcasted_iota(jnp.int32, (8, 128), 1)

    def reduce(step, t, diagonal):
        pair = block_of(step)[1] if step is not None else 7
        crosses = []
        for w in range(2):
            cross = None
            for g in range(8):
                block = t[w * 128 : (w + 1) * 128, g * 128 : (g + 1) * 128]
                turned = block.astype(jnp.bfloat16).T.astype(jnp.float32)
                one = jnp.sum((block * turned).reshape(16, 8, 128), axis=0)
                cross = one if cross is None else cross + one
                found = jnp.where(lane == row, block[0:8], 0.0)
                for k in range(1, 16):
                    found = jnp.where(lane == row + 8 * k, block[8 * k : 8 * k + 8], found)
                diagonal[(w * 8 + g) * 8 : (w * 8 + g) * 8 + 8, :] = found
            crosses.append(cross)
        lines = diagonal[pl.ds(0, 16, stride=8), :]
        for k in range(1, 8):
            lines = lines + diagonal[pl.ds(k, 16, stride=8), :]
        trace = jnp.sum(lines, axis=1, keepdims=True)
        squares = jnp.where(lax.broadcasted_iota(jnp.int32, (16, 128), 1) == 0, trace * trace, 0.0)
        for w in range(2):
            rows = pl.ds(pl.multiple_of((pair * 2 + w) * 8, 8), 8)
            acc[rows, :] = acc[rows, :] + squares[w * 8 : w * 8 + 8] - crosses[w]

    def relation(group):
        return ((group >> 2) ^ xl) * 4 + ((y - (group & 3)) & 3)

    def branch_in():
        arrived(*[f"branch{r}" for r in range(1, 8)])
        count = live[0, 0]
        for k in range(4):
            fresh[k] = inbox[jnp.where(k < count, relation(parents[k, walker] >> 2), 8)]
        pltpu.make_async_copy(fresh, new_hbm, load_sem.at[3]).start()

    def serve(step):
        @pl.when(step == 2)
        def _():
            arrived("core")

        @pl.when(step == 4)
        def _():
            arrived("hi0")
            start("sib16", "lo0", "y0")
            arrived("up0", "down0")
            propagate(early, wz.at[4:6])
            start("up4")

        @pl.when(step == 6)
        def _():
            arrived("up1", "down1", "hi1")
            start("up50", "up51", "down4", "sib17", "lo1", "y1")
            start("branch5", "branch2", "branch6", "branch7")

        @pl.when(step == 8)
        def _():
            arrived("up2", "down2", "hi2")
            start("down50", "down51", "sib24")
            arrived("y0", "lo0")
            start("sib18", "sib19")

        @pl.when(step == 10)
        def _():
            arrived("sib16", "sib17", "sib18", "sib19")

        @pl.when(step == 18)
        def _():
            arrived("sib24", "sib25", "sib26", "sib27")

        @pl.when(step == 24)
        def _():
            arrived("up4", "down4")

        @pl.when(step == 14)
        def _():
            arrived("up3", "down3", "hi3")
            start("sib25")
            arrived("y1", "lo1")
            start("sib26", "sib27")

    multiply(0, ta)
    multiply(1, tb)
    reduce(0, ta, da)

    def body(i, carry):
        step = 2 * i
        serve(step)
        multiply(step, ta)
        reduce(step - 1, tb, db)
        multiply(step + 1, tb)
        reduce(step, ta, da)
        return carry

    def sublane_sums(base, count):
        sums = acc[pl.ds(base * 8, count, stride=8), :]
        for k in range(1, 8):
            sums = sums + acc[pl.ds(base * 8 + k, count, stride=8), :]
        return sums

    lax.fori_loop(1, BLOCKS // 2 - 2, body, 0)
    reduce(BLOCKS - 5, tb, db)
    totals[...] = sublane_sums(0, 16)
    start("part0", "part1", "part2")
    own_e[...] = jnp.zeros_like(own_e)
    last[...] = jnp.zeros_like(last)
    def multiply_half(octet, half):
        columns = slice(half * 512, half * 512 + 512)
        out = lax.dot_general(
            wz[14:16, :, columns].reshape(256, 512),
            cv[octet * 8 : octet * 8 + 8, :, columns].reshape(1024, 512),
            (((1,), (1,)), ((), ())),
            preferred_element_type=jnp.float32,
        )
        t7[octet] = out if half == 0 else t7[octet] + out

    arrived("up50", "down50")
    for octet in range(4):
        multiply_half(octet, 0)
    arrived("up51", "down51")
    multiply_half(0, 1)
    for octet in range(4):
        if octet < 3:
            multiply_half(octet + 1, 1)
        reduce(None, t7.at[octet], db if octet % 2 else da)
    last[0:2, :] = sublane_sums(14, 2)
    start(*[f"last{r}" for r in range(8)])
    arrived("part0", "part1", "part2")
    for k in range(4):
        below, above = 4 + 2 * k, 5 + 2 * ((k + 3) % 4)
        line = totals[k : k + 1, :] + parts[1, below : below + 1, :] + parts[0, above : above + 1, :]
        if k % 2 == 0:
            line = line + parts[2, 12 + k // 2 : 13 + k // 2, :]
        own_e[k : k + 1, :] = line
    start(*[f"energy{r}" for r in range(1, 8)])
    branch_in()
    all_e[0] = own_e[...]
    arrived(*[f"energy{r}" for r in range(1, 8)])
    arrived(*[f"last{r}" for r in range(8)])
    count = live[0, 0]
    result = jnp.zeros((1, 128), jnp.float32)
    for k in range(4):
        place = parents[k, walker] & 3
        r = relation(parents[k, walker] >> 2)
        late = jnp.where((place & 1) == 1, place >> 1, 8)
        tile = jnp.where(row == place, all_e[r], 0.0) + jnp.where(row == late, lasts[r], 0.0)
        value = jnp.sum(jnp.sum(tile, axis=0, keepdims=True), axis=1, keepdims=True)
        chosen = (lane[0:1] == k) & (count > k)
        result = jnp.where(chosen, value * (0.5 / 16384), result)
    energy_ref[0] = result[:, 0:4]

    for name in table:
        copy(name).wait_send()
    pltpu.make_async_copy(fresh, new_hbm, load_sem.at[3]).wait()


def on_device(walkers, propagator, chol, parent_group, parent_slot, live_count):
    bf16, f32 = jnp.bfloat16, jnp.float32
    slot = (128, 1024)
    anywhere = pl.BlockSpec(memory_space=pl.ANY)
    hbm = pl.BlockSpec(memory_space=pltpu.HBM)
    parents = (parent_group * 4 + parent_slot)[:, 0, :].T
    routes = 56
    return pl.pallas_call(
        kernel,
        out_shape=(
            jax.ShapeDtypeStruct((4,) + slot, bf16),
            jax.ShapeDtypeStruct((1, 1, 4), f32),
        ),
        in_specs=[hbm] * 5,
        out_specs=(anywhere, pl.BlockSpec(memory_space=pltpu.VMEM)),
        scratch_shapes=[
            pltpu.SMEM((4, 8), jnp.int32),
            pltpu.SMEM((1, 1), jnp.int32),
            pltpu.VMEM((4,) + slot, bf16),
            pltpu.VMEM((2,) + slot, bf16),
            pltpu.VMEM((1024, 1024), bf16),
            pltpu.VMEM((4,) + slot, bf16),
            pltpu.VMEM((16,) + slot, bf16),
            pltpu.VMEM((32,) + slot, bf16),
            pltpu.VMEM((8,) + slot, bf16),
            pltpu.VMEM((9,) + slot, bf16),
            pltpu.VMEM((4,) + slot, bf16),
            pltpu.VMEM((256, 1024), f32),
            pltpu.VMEM((256, 1024), f32),
            pltpu.VMEM((4, 256, 1024), f32),
            pltpu.VMEM((128, 128), f32),
            pltpu.VMEM((128, 128), f32),
            pltpu.VMEM((128, 128), f32),
            pltpu.VMEM((16, 128), f32),
            pltpu.VMEM((3, 16, 128), f32),
            pltpu.VMEM((8, 128), f32),
            pltpu.VMEM((8, 8, 128), f32),
            pltpu.VMEM((8, 128), f32),
            pltpu.VMEM((8, 8, 128), f32),
            pltpu.SemaphoreType.DMA((7,)),
            pltpu.SemaphoreType.DMA((routes,)),
            pltpu.SemaphoreType.DMA((routes,)),
        ],
        compiler_params=pltpu.CompilerParams(
            collective_id=0, has_side_effects=True, vmem_limit_bytes=52 << 20
        ),
        cost_estimate=pl.CostEstimate(
            flops=2 * (512 * 128 * 128 * 1024 + 512 * 1024 * 1024),
            bytes_accessed=8 << 20,
            transcendentals=0,
        ),
        name="propagate_branch_energy",
    )(parents, live_count, walkers, propagator, chol)


def solution(mesh):
    in_specs = (
        P(("walker", "vec"), None, None),
        P(),
        P("vec", None, None),
        P(None, "vec", None),
        P(None, "vec", None),
        P("walker", "vec"),
    )
    out_specs = (P(("walker", "vec"), None, None), P("walker", "vec", None))
    return jax.shard_map(
        on_device, mesh=mesh, in_specs=in_specs, out_specs=out_specs, check_vma=False
    )
```

```python
import jax
import jax.numpy as jnp
from jax import lax
from jax.experimental import pallas as pl
from jax.experimental.pallas import tpu as pltpu
from jax.sharding import PartitionSpec as P

MESH = pl.DeviceIdType.MESH
BLOCKS = 32
PIECES = ((0, 1024),)
RELATIONS = [(across, along) for across in range(2) for along in range(4)]


def block_of(step):
    octet = step % 2
    pair = step // 2
    octet = jnp.where(step < 4, step // 2, octet)
    pair = jnp.where(step < 4, step % 2, pair)
    for first, last, kind, value in (
        (10, 15, "octet", 2),
        (15, 18, "pair", 5),
        (18, 24, "octet", 3),
        (24, 28, "pair", 6),
        (28, 32, "pair", 7),
    ):
        inside = (step >= first) & (step < last)
        octet = jnp.where(inside, value if kind == "octet" else step - first, octet)
        pair = jnp.where(inside, value if kind == "pair" else step - first, pair)
    return octet, pair


def kernel(
    groups_hbm, places_hbm, live_hbm, walkers_hbm, prop_hbm, chol_hbm, new_hbm, energy_ref,
    groups, places, live,
    raw, early, prop, moved, wz, cv, outbox, inbox, fresh, ta, tb, t7, da, db, acc,
    totals, parts, own_e, all_e, last, lasts, load_sem, send_sem, recv_sem,
):
    walker = lax.axis_index("walker")
    vec = lax.axis_index("vec")
    xl, y = walker // 4, walker % 4
    xh, z, core = vec // 8, (vec // 2) % 4, vec % 2

    def at(xl=xl, y=y, xh=xh, z=z, core=core):
        return (xl * 4 + y, (xh * 4 + z) * 2 + core)

    sibling = at(core=1 - core)
    hi = at(xl=1 - xl, xh=1 - xh)
    lo = at(xl=1 - xl)
    z_up, z_down, z_far = at(z=(z + 1) % 4), at(z=(z + 3) % 4), at(z=(z + 2) % 4)
    y_up, y_down = at(y=(y + 1) % 4), at(y=(y + 3) % 4)
    related = [
        at(xl=(xl + across) % 2, y=(y + along) % 4) for across, along in RELATIONS
    ]

    beyond = [
        at(xl=(xl + across) % 2, y=(y + along) % 4, z=(z + 2) % 4) for across, along in RELATIONS
    ]

    barrier = pltpu.get_barrier_semaphore()
    partners = [sibling, hi, z_up, z_down] + related[1:]
    for partner in partners:
        pl.semaphore_signal(barrier, inc=1, device_id=partner, device_id_type=MESH)

    small = [
        pltpu.make_async_copy(source, target, load_sem.at[4 + k])
        for k, (source, target) in enumerate(
            ((groups_hbm, groups), (places_hbm, places), (live_hbm, live))
        )
    ]
    load_prop = pltpu.make_async_copy(prop_hbm, prop, load_sem.at[0])
    load_raw = pltpu.make_async_copy(walkers_hbm, raw, load_sem.at[1])
    load_chol = pltpu.make_async_copy(chol_hbm, cv.at[pl.ds(0, 8)], load_sem.at[2])
    load_raw.start()
    load_prop.start()
    for load in small:
        load.start()
    load_chol.start()

    table = {}

    def route(name, source, target, device):
        table[name] = (len(table), source, target, device)

    first = (1 - xl) + 2 * (y % 2)
    second = 3 - first
    route("core", chol_hbm, cv.at[pl.ds(8, 8)], sibling)
    for k, (source, slot) in enumerate(
        ((2 * first, 16), (2 * first + 1, 17), (2 * second, 24), (2 * second + 1, 25))
    ):
        route(f"hi{k}", chol_hbm.at[pl.ds(source, 1)], cv.at[pl.ds(slot, 1)], hi)
    route("lo0", cv.at[pl.ds(16, 1)], cv.at[pl.ds(18, 1)], lo)
    route("lo1", cv.at[pl.ds(17, 1)], cv.at[pl.ds(26, 1)], lo)
    route("y0", cv.at[pl.ds(16, 1)], cv.at[pl.ds(19, 1)], y_up)
    route("y1", cv.at[pl.ds(17, 1)], cv.at[pl.ds(27, 1)], y_down)
    for slot in (16, 17, 18, 19, 24, 25, 26, 27):
        route(f"sib{slot}", cv.at[pl.ds(slot, 1)], cv.at[pl.ds(slot + 4, 1)], sibling)
    for k in range(4):
        if k == 0:
            route("up0", walkers_hbm.at[pl.ds(0, 1)], early.at[pl.ds(0, 1)], z_up)
            route("down0", walkers_hbm.at[pl.ds(1, 1)], early.at[pl.ds(1, 1)], z_down)
            continue
        route(f"up{k}", moved.at[pl.ds(k, 1)], wz.at[pl.ds(4 + 2 * k, 1)], z_up)
        route(f"down{k}", moved.at[pl.ds((k + 1) % 4, 1)], wz.at[pl.ds(5 + 2 * k, 1)], z_down)
    route("up4", wz.at[pl.ds(4, 1)], wz.at[pl.ds(12, 1)], z_up)
    route("down4", wz.at[pl.ds(7, 1)], wz.at[pl.ds(13, 1)], z_down)
    for part, (start_column, columns) in enumerate(PIECES):
        piece = pl.ds(start_column, columns)
        route(f"up5{part}", wz.at[pl.ds(6, 1), :, piece], wz.at[pl.ds(14, 1), :, piece], z_up)
        route(f"down5{part}", wz.at[pl.ds(9, 1), :, piece], wz.at[pl.ds(15, 1), :, piece], z_down)
    for r in range(1, 8):
        route(f"branch{r}", outbox.at[pl.ds(r, 1)], inbox.at[pl.ds(r, 1)], related[r])
    for k, device in enumerate((z_up, z_down, z_far)):
        route(f"part{k}", totals, parts.at[k], device)
    for r in range(1, 8):
        route(f"energy{r}", own_e, all_e.at[r], related[r])
    for r in range(8):
        route(f"last{r}", last, lasts.at[r], beyond[r])

    def copy(name):
        index, source, target, device = table[name]
        return pltpu.make_async_remote_copy(
            src_ref=source,
            dst_ref=target,
            send_sem=send_sem.at[index],
            recv_sem=recv_sem.at[index],
            device_id=device,
            device_id_type=MESH,
        )

    def start(*names):
        for name in names:
            copy(name).start()

    def arrived(*names):
        for name in names:
            copy(name).wait_recv()

    acc[...] = jnp.zeros_like(acc)
    inbox[8] = jnp.zeros_like(inbox[8])

    pl.semaphore_wait(barrier, len(partners))
    start("up0", "down0", "hi0", "hi1", "hi2", "hi3", "core")

    load_raw.wait()
    load_prop.wait()

    def propagate(source, *targets):
        rows = source[...].reshape(256, 1024)

        @pl.loop(0, 4)
        def _(tile):
            columns = pl.ds(pl.multiple_of(tile * 256, 256), 256)
            out = jnp.dot(rows, prop[:, columns], preferred_element_type=jnp.float32)
            out = out.astype(jnp.bfloat16).reshape(2, 128, 256)
            for target in targets:
                target[:, :, columns] = out

    propagate(raw.at[0:2], moved.at[0:2], wz.at[0:2])
    start("up1")
    propagate(raw.at[2:4], moved.at[2:4], wz.at[2:4])
    start("down1", "up2", "down2", "up3", "down3")

    for load in small:
        load.wait()

    def choose(r):
        across, along = RELATIONS[r]
        other = ((xl + across) % 2) * 4 + (y + along) % 4
        slot = 0
        for k in range(4):
            slot = slot + jnp.where(groups[k, other] == walker, places[k, other], 0)
        return moved[slot]

    for r in (4, 1, 3):
        outbox[r] = choose(r)
        start(f"branch{r}")
    for r in (2, 5, 6, 7):
        outbox[r] = choose(r)
    inbox[0] = choose(0)

    load_chol.wait()

    def multiply(step, t):
        octet, pair = block_of(step)
        vectors = cv[pl.ds(octet * 8, 8)].reshape(1024, 1024)
        block = wz[pl.ds(pair * 2, 2)].reshape(256, 1024)
        t[...] = lax.dot_general(
            block, vectors, (((1,), (1,)), ((), ())), preferred_element_type=jnp.float32
        )

    row = lax.broadcasted_iota(jnp.int32, (8, 128), 0)
    lane = lax.broadcasted_iota(jnp.int32, (8, 128), 1)

    def reduce(step, t, diagonal):
        pair = block_of(step)[1] if step is not None else 7
        crosses = []
        for w in range(2):
            cross = None
            for g in range(8):
                block = t[w * 128 : (w + 1) * 128, g * 128 : (g + 1) * 128]
                turned = block.astype(jnp.bfloat16).T.astype(jnp.float32)
                one = jnp.sum((block * turned).reshape(16, 8, 128), axis=0)
                cross = one if cross is None else cross + one
                found = jnp.where(lane == row, block[0:8], 0.0)
                for k in range(1, 16):
                    found = jnp.where(lane == row + 8 * k, block[8 * k : 8 * k + 8], found)
                diagonal[(w * 8 + g) * 8 : (w * 8 + g) * 8 + 8, :] = found
            crosses.append(cross)
        lines = diagonal[pl.ds(0, 16, stride=8), :]
        for k in range(1, 8):
            lines = lines + diagonal[pl.ds(k, 16, stride=8), :]
        trace = jnp.sum(lines, axis=1, keepdims=True)
        squares = jnp.where(lax.broadcasted_iota(jnp.int32, (16, 128), 1) == 0, trace * trace, 0.0)
        for w in range(2):
            rows = pl.ds(pl.multiple_of((pair * 2 + w) * 8, 8), 8)
            acc[rows, :] = acc[rows, :] + squares[w * 8 : w * 8 + 8] - crosses[w]

    def relation(group):
        return ((group >> 2) ^ xl) * 4 + ((y - (group & 3)) & 3)

    def branch_in():
        arrived(*[f"branch{r}" for r in range(1, 8)])
        count = live[0, 0]
        for k in range(4):
            fresh[k] = inbox[jnp.where(k < count, relation(groups[k, walker]), 8)]
        pltpu.make_async_copy(fresh, new_hbm, load_sem.at[3]).start()

    def serve(step):
        @pl.when(step == 2)
        def _():
            arrived("core")

        @pl.when(step == 4)
        def _():
            arrived("hi0")
            start("sib16", "lo0", "y0")
            arrived("up0", "down0")
            propagate(early, wz.at[4:6])
            start("up4")

        @pl.when(step == 6)
        def _():
            arrived("up1", "down1", "hi1")
            start(*[f"up5{part}" for part in range(len(PIECES))], "down4", "sib17", "lo1", "y1")
            start("branch5", "branch2", "branch6", "branch7")

        @pl.when(step == 8)
        def _():
            arrived("up2", "down2", "hi2")
            start(*[f"down5{part}" for part in range(len(PIECES))], "sib24")
            arrived("y0", "lo0")
            start("sib18", "sib19")

        @pl.when(step == 10)
        def _():
            arrived("sib16", "sib17", "sib18", "sib19")

        @pl.when(step == 18)
        def _():
            arrived("sib24", "sib25", "sib26", "sib27")

        @pl.when(step == 24)
        def _():
            arrived("up4", "down4")

        @pl.when(step == 14)
        def _():
            arrived("up3", "down3", "hi3")
            start("sib25")
            arrived("y1", "lo1")
            start("sib26", "sib27")

    multiply(0, ta)
    multiply(1, tb)
    reduce(0, ta, da)

    def body(i, carry):
        step = 2 * i
        serve(step)
        multiply(step, ta)
        reduce(step - 1, tb, db)
        multiply(step + 1, tb)
        reduce(step, ta, da)
        return carry

    def sublane_sums(base, count):
        sums = acc[pl.ds(base * 8, count, stride=8), :]
        for k in range(1, 8):
            sums = sums + acc[pl.ds(base * 8 + k, count, stride=8), :]
        return sums

    lax.fori_loop(1, BLOCKS // 2 - 2, body, 0)
    reduce(BLOCKS - 5, tb, db)
    totals[...] = sublane_sums(0, 16)
    start("part0", "part1", "part2")
    own_e[...] = jnp.zeros_like(own_e)
    last[...] = jnp.zeros_like(last)
    def multiply_piece(octet, part):
        start_column, count = PIECES[part]
        columns = slice(start_column, start_column + count)
        out = lax.dot_general(
            wz[14:16, :, columns].reshape(256, count),
            cv[octet * 8 : octet * 8 + 8, :, columns].reshape(1024, count),
            (((1,), (1,)), ((), ())),
            preferred_element_type=jnp.float32,
        )
        t7[octet] = out if part == 0 else t7[octet] + out

    final = len(PIECES) - 1
    for part in range(final):
        arrived(f"up5{part}", f"down5{part}")
        for octet in range(4):
            multiply_piece(octet, part)
    arrived(f"up5{final}", f"down5{final}")
    multiply_piece(0, final)
    for octet in range(4):
        if octet < 3:
            multiply_piece(octet + 1, final)
        reduce(None, t7.at[octet], db if octet % 2 else da)
    last[0:2, :] = sublane_sums(14, 2)
    start(*[f"last{r}" for r in range(8)])
    arrived("part0", "part1", "part2")
    for k in range(4):
        below, above = 4 + 2 * k, 5 + 2 * ((k + 3) % 4)
        line = totals[k : k + 1, :] + parts[1, below : below + 1, :] + parts[0, above : above + 1, :]
        if k % 2 == 0:
            line = line + parts[2, 12 + k // 2 : 13 + k // 2, :]
        own_e[k : k + 1, :] = line
    start(*[f"energy{r}" for r in range(1, 8)])
    branch_in()
    all_e[0] = own_e[...]
    arrived(*[f"energy{r}" for r in range(1, 8)])
    arrived(*[f"last{r}" for r in range(8)])
    count = live[0, 0]
    result = jnp.zeros((1, 128), jnp.float32)
    for k in range(4):
        place = places[k, walker]
        r = relation(groups[k, walker])
        late = jnp.where((place & 1) == 1, place >> 1, 8)
        tile = jnp.where(row == place, all_e[r], 0.0) + jnp.where(row == late, lasts[r], 0.0)
        value = jnp.sum(jnp.sum(tile, axis=0, keepdims=True), axis=1, keepdims=True)
        chosen = (lane[0:1] == k) & (count > k)
        result = jnp.where(chosen, value * (0.5 / 16384), result)
    energy_ref[0] = result[:, 0:4]

    for name in table:
        copy(name).wait_send()
    pltpu.make_async_copy(fresh, new_hbm, load_sem.at[3]).wait()


def on_device(walkers, propagator, chol, parent_group, parent_slot, live_count):
    bf16, f32 = jnp.bfloat16, jnp.float32
    slot = (128, 1024)
    anywhere = pl.BlockSpec(memory_space=pl.ANY)
    hbm = pl.BlockSpec(memory_space=pltpu.HBM)
    operands = [
        one if one is live_count else pltpu.with_memory_space_constraint(one, pltpu.HBM)
        for one in (
            parent_group[:, 0, :].T, parent_slot[:, 0, :].T, live_count, walkers, propagator, chol
        )
    ]
    routes = 64
    return pl.pallas_call(
        kernel,
        out_shape=(
            jax.ShapeDtypeStruct((4,) + slot, bf16),
            jax.ShapeDtypeStruct((1, 1, 4), f32),
        ),
        in_specs=[hbm] * 6,
        out_specs=(anywhere, pl.BlockSpec(memory_space=pltpu.VMEM)),
        scratch_shapes=[
            pltpu.SMEM((4, 8), jnp.int32),
            pltpu.SMEM((4, 8), jnp.int32),
            pltpu.SMEM((1, 1), jnp.int32),
            pltpu.VMEM((4,) + slot, bf16),
            pltpu.VMEM((2,) + slot, bf16),
            pltpu.VMEM((1024, 1024), bf16),
            pltpu.VMEM((4,) + slot, bf16),
            pltpu.VMEM((16,) + slot, bf16),
            pltpu.VMEM((32,) + slot, bf16),
            pltpu.VMEM((8,) + slot, bf16),
            pltpu.VMEM((9,) + slot, bf16),
            pltpu.VMEM((4,) + slot, bf16),
            pltpu.VMEM((256, 1024), f32),
            pltpu.VMEM((256, 1024), f32),
            pltpu.VMEM((4, 256, 1024), f32),
            pltpu.VMEM((128, 128), f32),
            pltpu.VMEM((128, 128), f32),
            pltpu.VMEM((128, 128), f32),
            pltpu.VMEM((16, 128), f32),
            pltpu.VMEM((3, 16, 128), f32),
            pltpu.VMEM((8, 128), f32),
            pltpu.VMEM((8, 8, 128), f32),
            pltpu.VMEM((8, 128), f32),
            pltpu.VMEM((8, 8, 128), f32),
            pltpu.SemaphoreType.DMA((7,)),
            pltpu.SemaphoreType.DMA((routes,)),
            pltpu.SemaphoreType.DMA((routes,)),
        ],
        compiler_params=pltpu.CompilerParams(
            collective_id=0, has_side_effects=True, vmem_limit_bytes=52 << 20
        ),
        cost_estimate=pl.CostEstimate(
            flops=2 * (512 * 128 * 128 * 1024 + 512 * 1024 * 1024),
            bytes_accessed=8 << 20,
            transcendentals=0,
        ),
        name="propagate_branch_energy",
    )(*operands)


def solution(mesh):
    in_specs = (
        P(("walker", "vec"), None, None),
        P(),
        P("vec", None, None),
        P(None, "vec", None),
        P(None, "vec", None),
        P("walker", "vec"),
    )
    out_specs = (P(("walker", "vec"), None, None), P("walker", "vec", None))
    return jax.shard_map(
        on_device, mesh=mesh, in_specs=in_specs, out_specs=out_specs, check_vma=False
    )
```

```python
import jax
import jax.numpy as jnp
from jax import lax
from jax.experimental import pallas as pl
from jax.experimental.pallas import tpu as pltpu
from jax.sharding import PartitionSpec as P

MESH = pl.DeviceIdType.MESH
BLOCKS = 32
PIECES = ((0, 1024),)
FAR_FIRST = (6, 2, 5, 7, 1, 3, 4, 0)
RELATIONS = [(across, along) for across in range(2) for along in range(4)]


def block_of(step):
    octet = step % 2
    pair = step // 2
    octet = jnp.where(step < 4, step // 2, octet)
    pair = jnp.where(step < 4, step % 2, pair)
    for first, last, kind, value in (
        (10, 15, "octet", 2),
        (15, 18, "pair", 5),
        (18, 24, "octet", 3),
        (24, 28, "pair", 6),
        (28, 32, "pair", 7),
    ):
        inside = (step >= first) & (step < last)
        octet = jnp.where(inside, value if kind == "octet" else step - first, octet)
        pair = jnp.where(inside, value if kind == "pair" else step - first, pair)
    return octet, pair


def kernel(
    groups_hbm, places_hbm, live_hbm, walkers_hbm, prop_hbm, chol_hbm, new_hbm, energy_ref,
    groups, places, live,
    raw, early, prop, moved, wz, cv, outbox, inbox, fresh, ta, tb, t7, da, db, acc,
    totals, parts, own_e, all_e, last, lasts, load_sem, send_sem, recv_sem,
):
    walker = lax.axis_index("walker")
    vec = lax.axis_index("vec")
    xl, y = walker // 4, walker % 4
    xh, z, core = vec // 8, (vec // 2) % 4, vec % 2

    def at(xl=xl, y=y, xh=xh, z=z, core=core):
        return (xl * 4 + y, (xh * 4 + z) * 2 + core)

    sibling = at(core=1 - core)
    hi = at(xl=1 - xl, xh=1 - xh)
    lo = at(xl=1 - xl)
    z_up, z_down, z_far = at(z=(z + 1) % 4), at(z=(z + 3) % 4), at(z=(z + 2) % 4)
    y_up, y_down = at(y=(y + 1) % 4), at(y=(y + 3) % 4)
    related = [
        at(xl=(xl + across) % 2, y=(y + along) % 4) for across, along in RELATIONS
    ]

    beyond = [
        at(xl=(xl + across) % 2, y=(y + along) % 4, z=(z + 2) % 4) for across, along in RELATIONS
    ]

    barrier = pltpu.get_barrier_semaphore()
    partners = [related[r] for r in FAR_FIRST if r] + [z_up, z_down, hi, sibling]
    for partner in partners:
        pl.semaphore_signal(barrier, inc=1, device_id=partner, device_id_type=MESH)

    small = [
        pltpu.make_async_copy(source, target, load_sem.at[4 + k])
        for k, (source, target) in enumerate(
            ((groups_hbm, groups), (places_hbm, places), (live_hbm, live))
        )
    ]
    load_prop = pltpu.make_async_copy(prop_hbm, prop, load_sem.at[0])
    load_raw = pltpu.make_async_copy(walkers_hbm, raw, load_sem.at[1])
    load_chol = pltpu.make_async_copy(chol_hbm, cv.at[pl.ds(0, 8)], load_sem.at[2])
    load_raw.start()
    load_prop.start()
    for load in small:
        load.start()
    load_chol.start()

    table = {}

    def route(name, source, target, device):
        table[name] = (len(table), source, target, device)

    first = (1 - xl) + 2 * (y % 2)
    second = 3 - first
    route("core", chol_hbm, cv.at[pl.ds(8, 8)], sibling)
    for k, (source, slot) in enumerate(
        ((2 * first, 16), (2 * first + 1, 17), (2 * second, 24), (2 * second + 1, 25))
    ):
        route(f"hi{k}", chol_hbm.at[pl.ds(source, 1)], cv.at[pl.ds(slot, 1)], hi)
    route("lo0", cv.at[pl.ds(16, 1)], cv.at[pl.ds(18, 1)], lo)
    route("lo1", cv.at[pl.ds(17, 1)], cv.at[pl.ds(26, 1)], lo)
    route("y0", cv.at[pl.ds(16, 1)], cv.at[pl.ds(19, 1)], y_up)
    route("y1", cv.at[pl.ds(17, 1)], cv.at[pl.ds(27, 1)], y_down)
    for slot in (16, 17, 18, 19, 24, 25, 26, 27):
        route(f"sib{slot}", cv.at[pl.ds(slot, 1)], cv.at[pl.ds(slot + 4, 1)], sibling)
    for k in range(4):
        if k == 0:
            route("up0", walkers_hbm.at[pl.ds(0, 1)], early.at[pl.ds(0, 1)], z_up)
            route("down0", walkers_hbm.at[pl.ds(1, 1)], early.at[pl.ds(1, 1)], z_down)
            continue
        route(f"up{k}", moved.at[pl.ds(k, 1)], wz.at[pl.ds(4 + 2 * k, 1)], z_up)
        route(f"down{k}", moved.at[pl.ds((k + 1) % 4, 1)], wz.at[pl.ds(5 + 2 * k, 1)], z_down)
    route("up4", wz.at[pl.ds(4, 1)], wz.at[pl.ds(12, 1)], z_up)
    route("down4", wz.at[pl.ds(7, 1)], wz.at[pl.ds(13, 1)], z_down)
    for part, (start_column, columns) in enumerate(PIECES):
        piece = pl.ds(start_column, columns)
        route(f"up5{part}", wz.at[pl.ds(6, 1), :, piece], wz.at[pl.ds(14, 1), :, piece], z_up)
        route(f"down5{part}", wz.at[pl.ds(9, 1), :, piece], wz.at[pl.ds(15, 1), :, piece], z_down)
    for r in range(1, 8):
        route(f"branch{r}", outbox.at[pl.ds(r, 1)], inbox.at[pl.ds(r, 1)], related[r])
    for k, device in enumerate((z_up, z_down, z_far)):
        route(f"part{k}", totals, parts.at[k], device)
    for r in range(1, 8):
        route(f"energy{r}", own_e, all_e.at[r], related[r])
    for r in range(8):
        route(f"last{r}", last, lasts.at[r], beyond[r])

    def copy(name):
        index, source, target, device = table[name]
        return pltpu.make_async_remote_copy(
            src_ref=source,
            dst_ref=target,
            send_sem=send_sem.at[index],
            recv_sem=recv_sem.at[index],
            device_id=device,
            device_id_type=MESH,
        )

    def start(*names):
        for name in names:
            copy(name).start()

    def arrived(*names):
        for name in names:
            copy(name).wait_recv()

    acc[...] = jnp.zeros_like(acc)
    inbox[8] = jnp.zeros_like(inbox[8])

    pl.semaphore_wait(barrier, len(partners))
    start("up0", "down0", "hi0", "hi1", "hi2", "hi3", "core")

    load_raw.wait()
    load_prop.wait()

    def propagate(source, *targets):
        rows = source[...].reshape(256, 1024)

        @pl.loop(0, 4)
        def _(tile):
            columns = pl.ds(pl.multiple_of(tile * 256, 256), 256)
            out = jnp.dot(rows, prop[:, columns], preferred_element_type=jnp.float32)
            out = out.astype(jnp.bfloat16).reshape(2, 128, 256)
            for target in targets:
                target[:, :, columns] = out

    propagate(raw.at[0:2], moved.at[0:2], wz.at[0:2])
    start("up1")
    propagate(raw.at[2:4], moved.at[2:4], wz.at[2:4])
    start("down1")

    for load in small:
        load.wait()

    def choose(r):
        across, along = RELATIONS[r]
        other = ((xl + across) % 2) * 4 + (y + along) % 4
        slot = 0
        for k in range(4):
            slot = slot + jnp.where(groups[k, other] == walker, places[k, other], 0)
        return moved[slot]

    for r in (4, 1, 3):
        outbox[r] = choose(r)
        start(f"branch{r}")
    for r in (2, 5, 6, 7):
        outbox[r] = choose(r)
    inbox[0] = choose(0)

    load_chol.wait()

    def multiply(step, t):
        octet, pair = block_of(step)
        vectors = cv[pl.ds(octet * 8, 8)].reshape(1024, 1024)
        block = wz[pl.ds(pair * 2, 2)].reshape(256, 1024)
        t[...] = lax.dot_general(
            block, vectors, (((1,), (1,)), ((), ())), preferred_element_type=jnp.float32
        )

    row = lax.broadcasted_iota(jnp.int32, (8, 128), 0)
    lane = lax.broadcasted_iota(jnp.int32, (8, 128), 1)

    def reduce(step, t, diagonal):
        pair = block_of(step)[1] if step is not None else 7
        crosses = []
        for w in range(2):
            cross = None
            for g in range(8):
                block = t[w * 128 : (w + 1) * 128, g * 128 : (g + 1) * 128]
                turned = block.astype(jnp.bfloat16).T.astype(jnp.float32)
                one = jnp.sum((block * turned).reshape(16, 8, 128), axis=0)
                cross = one if cross is None else cross + one
                found = jnp.where(lane == row, block[0:8], 0.0)
                for k in range(1, 16):
                    found = jnp.where(lane == row + 8 * k, block[8 * k : 8 * k + 8], found)
                diagonal[(w * 8 + g) * 8 : (w * 8 + g) * 8 + 8, :] = found
            crosses.append(cross)
        lines = diagonal[pl.ds(0, 16, stride=8), :]
        for k in range(1, 8):
            lines = lines + diagonal[pl.ds(k, 16, stride=8), :]
        trace = jnp.sum(lines, axis=1, keepdims=True)
        squares = jnp.where(lax.broadcasted_iota(jnp.int32, (16, 128), 1) == 0, trace * trace, 0.0)
        for w in range(2):
            rows = pl.ds(pl.multiple_of((pair * 2 + w) * 8, 8), 8)
            acc[rows, :] = acc[rows, :] + squares[w * 8 : w * 8 + 8] - crosses[w]

    def relation(group):
        return ((group >> 2) ^ xl) * 4 + ((y - (group & 3)) & 3)

    def branch_in():
        arrived(*[f"branch{r}" for r in range(1, 8)])
        count = live[0, 0]
        for k in range(4):
            fresh[k] = inbox[jnp.where(k < count, relation(groups[k, walker]), 8)]
        pltpu.make_async_copy(fresh, new_hbm, load_sem.at[3]).start()

    def serve(step):
        @pl.when(step == 2)
        def _():
            arrived("core")

        @pl.when(step == 4)
        def _():
            arrived("hi0")
            start("sib16", "lo0", "y0", "up2", "down2")
            arrived("up0", "down0")
            propagate(early, wz.at[4:6])

        @pl.when(step == 6)
        def _():
            arrived("up1", "down1", "hi1")
            start("sib17", "lo1", "y1", "up3", "down3")

        @pl.when(step == 8)
        def _():
            arrived("up2", "down2", "hi2")
            start("sib24", "up4", "down4")
            for part in range(len(PIECES)):
                start(f"up5{part}", f"down5{part}")
            start("branch5", "branch2", "branch6", "branch7")
            arrived("y0", "lo0")
            start("sib18", "sib19")

        @pl.when(step == 10)
        def _():
            arrived("sib16", "sib17", "sib18", "sib19")

        @pl.when(step == 18)
        def _():
            arrived("sib24", "sib25", "sib26", "sib27")

        @pl.when(step == 24)
        def _():
            arrived("up4", "down4")

        @pl.when(step == 14)
        def _():
            arrived("up3", "down3", "hi3")
            start("sib25")
            arrived("y1", "lo1")
            start("sib26", "sib27")

    multiply(0, ta)
    multiply(1, tb)
    reduce(0, ta, da)

    def body(i, carry):
        step = 2 * i
        serve(step)
        multiply(step, ta)
        reduce(step - 1, tb, db)
        multiply(step + 1, tb)
        reduce(step, ta, da)
        return carry

    def sublane_sums(base, count):
        sums = acc[pl.ds(base * 8, count, stride=8), :]
        for k in range(1, 8):
            sums = sums + acc[pl.ds(base * 8 + k, count, stride=8), :]
        return sums

    lax.fori_loop(1, BLOCKS // 2 - 2, body, 0)
    own_e[...] = jnp.zeros_like(own_e)
    last[...] = jnp.zeros_like(last)
    def multiply_piece(octet, part):
        start_column, count = PIECES[part]
        columns = slice(start_column, start_column + count)
        out = lax.dot_general(
            wz[14:16, :, columns].reshape(256, count),
            cv[octet * 8 : octet * 8 + 8, :, columns].reshape(1024, count),
            (((1,), (1,)), ((), ())),
            preferred_element_type=jnp.float32,
        )
        t7[octet] = out if part == 0 else t7[octet] + out

    final = len(PIECES) - 1
    for part in range(final):
        arrived(f"up5{part}", f"down5{part}")
        for octet in range(4):
            multiply_piece(octet, part)
    arrived(f"up5{final}", f"down5{final}")
    multiply_piece(0, final)
    reduce(BLOCKS - 5, tb, db)
    totals[...] = sublane_sums(0, 16)
    start("part2", "part0", "part1")
    for octet in range(4):
        if octet < 3:
            multiply_piece(octet + 1, final)
        reduce(None, t7.at[octet], db if octet % 2 else da)
    last[0:2, :] = sublane_sums(14, 2)
    start(*[f"last{r}" for r in FAR_FIRST])
    arrived("part0", "part1", "part2")
    for k in range(4):
        below, above = 4 + 2 * k, 5 + 2 * ((k + 3) % 4)
        line = totals[k : k + 1, :] + parts[1, below : below + 1, :] + parts[0, above : above + 1, :]
        if k % 2 == 0:
            line = line + parts[2, 12 + k // 2 : 13 + k // 2, :]
        own_e[k : k + 1, :] = line
    start(*[f"energy{r}" for r in FAR_FIRST if r])
    branch_in()
    all_e[0] = own_e[...]
    arrived(*[f"energy{r}" for r in range(1, 8)])
    arrived(*[f"last{r}" for r in range(8)])
    count = live[0, 0]
    result = jnp.zeros((1, 128), jnp.float32)
    for k in range(4):
        place = places[k, walker]
        r = relation(groups[k, walker])
        late = jnp.where((place & 1) == 1, place >> 1, 8)
        tile = jnp.where(row == place, all_e[r], 0.0) + jnp.where(row == late, lasts[r], 0.0)
        value = jnp.sum(jnp.sum(tile, axis=0, keepdims=True), axis=1, keepdims=True)
        chosen = (lane[0:1] == k) & (count > k)
        result = jnp.where(chosen, value * (0.5 / 16384), result)
    energy_ref[0] = result[:, 0:4]

    for name in table:
        copy(name).wait_send()
    pltpu.make_async_copy(fresh, new_hbm, load_sem.at[3]).wait()


def on_device(walkers, propagator, chol, parent_group, parent_slot, live_count):
    bf16, f32 = jnp.bfloat16, jnp.float32
    slot = (128, 1024)
    anywhere = pl.BlockSpec(memory_space=pl.ANY)
    hbm = pl.BlockSpec(memory_space=pltpu.HBM)
    operands = [
        one if one is live_count else pltpu.with_memory_space_constraint(one, pltpu.HBM)
        for one in (
            parent_group[:, 0, :].T, parent_slot[:, 0, :].T, live_count, walkers, propagator, chol
        )
    ]
    routes = 64
    return pl.pallas_call(
        kernel,
        out_shape=(
            jax.ShapeDtypeStruct((4,) + slot, bf16),
            jax.ShapeDtypeStruct((1, 1, 4), f32),
        ),
        in_specs=[hbm] * 6,
        out_specs=(anywhere, pl.BlockSpec(memory_space=pltpu.VMEM)),
        scratch_shapes=[
            pltpu.SMEM((4, 8), jnp.int32),
            pltpu.SMEM((4, 8), jnp.int32),
            pltpu.SMEM((1, 1), jnp.int32),
            pltpu.VMEM((4,) + slot, bf16),
            pltpu.VMEM((2,) + slot, bf16),
            pltpu.VMEM((1024, 1024), bf16),
            pltpu.VMEM((4,) + slot, bf16),
            pltpu.VMEM((16,) + slot, bf16),
            pltpu.VMEM((32,) + slot, bf16),
            pltpu.VMEM((8,) + slot, bf16),
            pltpu.VMEM((9,) + slot, bf16),
            pltpu.VMEM((4,) + slot, bf16),
            pltpu.VMEM((256, 1024), f32),
            pltpu.VMEM((256, 1024), f32),
            pltpu.VMEM((4, 256, 1024), f32),
            pltpu.VMEM((128, 128), f32),
            pltpu.VMEM((128, 128), f32),
            pltpu.VMEM((128, 128), f32),
            pltpu.VMEM((16, 128), f32),
            pltpu.VMEM((3, 16, 128), f32),
            pltpu.VMEM((8, 128), f32),
            pltpu.VMEM((8, 8, 128), f32),
            pltpu.VMEM((8, 128), f32),
            pltpu.VMEM((8, 8, 128), f32),
            pltpu.SemaphoreType.DMA((7,)),
            pltpu.SemaphoreType.DMA((routes,)),
            pltpu.SemaphoreType.DMA((routes,)),
        ],
        compiler_params=pltpu.CompilerParams(
            collective_id=0, has_side_effects=True, vmem_limit_bytes=52 << 20
        ),
        cost_estimate=pl.CostEstimate(
            flops=2 * (512 * 128 * 128 * 1024 + 512 * 1024 * 1024),
            bytes_accessed=8 << 20,
            transcendentals=0,
        ),
        name="propagate_branch_energy",
    )(*operands)


def solution(mesh):
    in_specs = (
        P(("walker", "vec"), None, None),
        P(),
        P("vec", None, None),
        P(None, "vec", None),
        P(None, "vec", None),
        P("walker", "vec"),
    )
    out_specs = (P(("walker", "vec"), None, None), P("walker", "vec", None))
    return jax.shard_map(
        on_device, mesh=mesh, in_specs=in_specs, out_specs=out_specs, check_vma=False
    )
```
